32 devices in a mesh: seq: 4 (over y, x), tensor: 8 (over z, core).
Axes of the slice: x: 2, y: 2, z: 4, core: 2. Of those that a mesh axis runs over, the one named last changes fastest.
Arguments:
- hidden: bfloat16 [64, 2048], P('seq', 'tensor'), may hold values from -6 to 6
- router_logits: float32 [64, 8], replicated, may hold values from -6 to 6
- routes: int32 [64, 2], replicated, may hold values from 0 to 7, all different within a row
- w_query: bfloat16 [8, 2048, 2048], P(None, 'tensor', 'seq'), may hold values from -0.125 to 0.125
- w_keyval: bfloat16 [2048, 2, 2048], P('tensor', None, 'seq'), may hold values from -0.125 to 0.125
- w_output: bfloat16 [8, 2048, 2048], P(None, 'seq', 'tensor'), may hold values from -0.125 to 0.125
- k_cache: bfloat16 [1024, 64, 2048], P(('seq', 'tensor')), may hold values from -720 to 720
- v_cache: bfloat16 [1024, 64, 2048], P(('seq', 'tensor')), may hold values from -6 to 6
- lengths: int32 [16], replicated, may hold values from 1 to 4096, 26214 in all
- page_table: int32 [16, 64], replicated, may hold values from 0 to 31, as said below
- home_device: int32 [16], replicated, may hold values from 0 to 3
- accepted: int32 [16], replicated, may hold values from 1 to 4
Outputs:
- attn_out: float32 [64, 2048], P('seq', 'tensor')
- new_keys: float32 [64, 2048], P('tensor', 'seq')
- new_values: float32 [64, 2048], P('tensor', 'seq')
The draws below stay inside these ranges and needn't reach their ends.
Inputs may be any that keep to these rules, and one draw needn't show every extreme that they name: `page_table`: for each index s of seq and t of tensor, the pages j of the requests r with r // 2 = t and (home_device[r] + j) % 4 = s have distinct values.
All inputs are finite; a program needn't handle non-finite values.
Results may differ from the reference program's by a relative error of at most 0.019.
Values may be sent and summed in bfloat16 or wider, within the bound.
No kernel may reach another device: no remote copies, remote signals or barrier semaphores. Data moves between devices by JAX's collectives and lax.ppermute only.
A program may use at most 128 MiB of HBM per device.

```python
import math
import jax
import jax.numpy as jnp
import numpy as np
from jax import lax

D = 2048
E = 8
KVH = 16
HD = 128
Q = 4
PAGE = 64
MAXLEN = 4096
REQ_DEV = 2
REQ = 16
TOK = 64
MAXP = 64
PAGES_DEV = 16
SLOTS_DEV = 32
SLOTS = 1024
N_SEQ = 4
N_TENSOR = 8


def placement_helper(key):
    seq_devs = MAXP // PAGES_DEV
    tensor_devs = REQ // REQ_DEV
    shuffled = jax.random.permutation(jax.random.fold_in(key, 11), REQ)
    home_dev = (shuffled % seq_devs).astype(jnp.int32)
    slot_keys = jax.random.split(jax.random.fold_in(key, 23), tensor_devs * seq_devs)
    slot_orders = jax.vmap(lambda subkey: jax.random.permutation(subkey, SLOTS_DEV))(slot_keys)
    request_ids = jnp.arange(REQ, dtype=jnp.int32)[:, None]
    page_ids = jnp.arange(MAXP, dtype=jnp.int32)[None, :]
    seq_dev = (home_dev[:, None] + page_ids) % seq_devs
    tensor_dev = request_ids // REQ_DEV
    local_slot = request_ids % REQ_DEV * PAGES_DEV + page_ids // seq_devs
    slot_table = slot_orders[tensor_dev * seq_devs + seq_dev, local_slot]
    return (home_dev, slot_table.astype(jnp.int32))


def draw_home_device(key, part):
    return placement_helper(key)[0]


def draw_page_table(key, part):
    return placement_helper(key)[1]


def draw_k_cache(key, part):
    base_draw = jnp.clip(jax.random.normal(key, (SLOTS, PAGE, KVH * HD), jnp.float32), -6.0, 6.0)
    return base_draw.astype(jnp.bfloat16)


def with_ends(values, own_key, least, largest):
    index_at = [jax.random.randint(jax.random.fold_in(own_key, axis), (), 0, length) for axis, length in enumerate(values.shape)]
    main_axis = values.shape.index(max(values.shape))
    neighbour = index_at[:main_axis] + [(index_at[main_axis] + 1) % values.shape[main_axis]] + index_at[main_axis + 1:]
    return values.at[tuple(index_at)].set(least).at[tuple(neighbour)].set(largest)


def block_levels(stream_key, dims, shards, least, high):
    def one(position, parts):
        steps = jax.random.uniform(jax.random.fold_in(jax.random.fold_in(stream_key, 6), position), (parts,), jnp.float32, least / len(shards), high / len(shards))
        return jnp.repeat(jnp.exp(steps), dims[position] // parts).reshape((-1,) + (1,) * (len(dims) - position - 1))

    loudness = one(*shards[0])
    for cut in shards[1:]:
        loudness = loudness * one(*cut)
    return loudness


def picks_of(own_key, rows, amount, top, lift):
    order = jax.random.permutation(jax.random.fold_in(own_key, 1), amount)
    pull = order
    for power in range(3):
        pull = pull * pull // amount
    pull = pull * lift // amount
    lots = jax.random.randint(jax.random.fold_in(own_key, 2), (rows, amount), 0, 4096) + pull
    holders = jax.random.permutation(jax.random.fold_in(own_key, 3), rows)[jnp.arange(amount) % rows]
    lots = jnp.where(jnp.arange(rows)[:, None] == holders[None, :], 1 << 14, lots)
    merit = lots * amount + jnp.arange(amount)
    return lax.top_k(merit.astype(jnp.int32), top)[1].astype(jnp.int32)


def profile(number_of, total, most, slope):
    portions = [(1 << 20) // math.isqrt(standing ** slope) + 1 for standing in range(2, number_of + 1)]
    surplus, holding = total - most - (number_of - 1), [1] * (number_of - 1)
    while surplus > 0:
        free = [i for i in range(number_of - 1) if holding[i] < most]
        mass, left = sum([portions[i] for i in free]), surplus
        for i in free:
            addition = min(most - holding[i], max(1, left * portions[i] // mass), surplus)
            holding[i] = holding[i] + addition
            surplus = surplus - addition
    return np.array([most] + holding)


def uneven_parts(own_key, count, total, reach, lean):
    if count == 2:
        one = jax.random.randint(own_key, (), max(1, total - reach), min(reach, total - 1) + 1)
        return jnp.stack([one, total - one])
    sizes = jnp.asarray(profile(count, total, reach, lean), jnp.int32)
    pairs = (count - 1) // 2
    source_of, taker = sizes[1:1 + 2 * pairs:2], sizes[2:2 + 2 * pairs:2]
    margin = jnp.minimum(source_of - 1, reach - taker)
    shifted = jax.random.randint(jax.random.fold_in(own_key, 1), (pairs,), 0, 1 << 20) % (margin + 1)
    sizes = sizes.at[1:1 + 2 * pairs:2].set(source_of - shifted).at[2:2 + 2 * pairs:2].set(taker + shifted)
    return sizes[jax.random.permutation(jax.random.fold_in(own_key, 2), count)]


def noise(own_key, dims, spread, limit, cuts=(), held_as=jnp.bfloat16):
    level = block_levels(own_key, dims, cuts, -0.22, 0.18) if cuts else 1.0
    result = jax.random.normal(own_key, dims, jnp.float32) * spread * level
    return jnp.minimum(jnp.maximum(result, -limit), limit).astype(held_as)


def setup_inputs(seed: int = 0) -> dict:
    streams_of = jax.random.split(jax.random.key(seed), 13)
    hidden = noise(streams_of[0], (TOK, D), 1.0, 6.0, ((0, 4), (1, 8)))
    router_logits = noise(streams_of[1], (TOK, E), 1.5, 6.0, (), jnp.float32)
    routes = picks_of(streams_of[2], TOK, E, 2, 2048)
    w_query = noise(streams_of[3], (E, D, KVH * HD), D ** -0.5, 0.125, ((1, 8), (2, 4)))
    w_keyval = noise(streams_of[4], (D, 2, KVH * HD), D ** -0.5, 0.125, ((0, 8), (2, 4)))
    w_output = noise(streams_of[5], (E, KVH * HD, D), (KVH * HD) ** -0.5, 0.125, ((1, 4), (2, 8)))
    k_cache = draw_k_cache(jax.random.fold_in(streams_of[12], 71), 0)
    v_cache = noise(streams_of[7], (SLOTS, PAGE, KVH * HD), 1.0, 6.0, ((0, 32),))
    lengths = uneven_parts(streams_of[8], REQ, REQ * MAXLEN * 2 // 5, MAXLEN, 2).astype(jnp.int32)
    page_table = draw_page_table(jax.random.fold_in(streams_of[12], 71), 0)
    home_device = draw_home_device(jax.random.fold_in(streams_of[12], 71), 0)
    accepted = with_ends(jax.random.randint(streams_of[11], (REQ,), 1, Q + 1), jax.random.fold_in(streams_of[11], 1), 1, Q).astype(jnp.int32)
    return dict(hidden=hidden, router_logits=router_logits, routes=routes, w_query=w_query, w_keyval=w_keyval, w_output=w_output, k_cache=k_cache, v_cache=v_cache, lengths=lengths, page_table=page_table, home_device=home_device, accepted=accepted)


THETA = 10000.0

def rotate(vectors, positions):
    half_width = HD // 2
    inverse = THETA ** (-(jnp.arange(half_width, dtype=jnp.float32) * 2.0 / HD))
    angles = positions.astype(jnp.float32)[..., None] * inverse
    cosine = jnp.cos(angles)
    sine_vals = jnp.sin(angles)
    front_half = vectors[..., :half_width]
    back_half = vectors[..., half_width:]
    return jnp.concatenate([front_half * cosine - back_half * sine_vals, back_half * cosine + front_half * sine_vals], axis=-1)

def reference(hidden, router_logits, routes, w_query, w_keyval, w_output, k_cache, v_cache, lengths, page_table, home_device, accepted):
    tokens = hidden.shape[0]
    selector = routes[:, :, None] == jnp.arange(E, dtype=jnp.int32)[None, None, :]
    hidden_wide = hidden.astype(jnp.float32)
    query_every = jnp.einsum('nd,edh->neh', hidden_wide, w_query.astype(jnp.float32))
    query_two = lax.optimization_barrier(jnp.sum(jnp.where(selector[:, :, :, None], query_every[:, None, :, :], 0.0), axis=2))
    keyval = jnp.einsum('nd,dch->nch', hidden_wide, w_keyval.astype(jnp.float32))
    request_of = jnp.arange(tokens, dtype=jnp.int32) // Q
    step_of = jnp.arange(tokens, dtype=jnp.int32) % Q
    positions = lengths[request_of] + step_of
    queries = rotate(query_two.reshape(tokens, 2, KVH, HD), positions[:, None, None]).astype(jnp.bfloat16)
    keys_rotated = rotate(keyval[:, 0].reshape(tokens, KVH, HD), positions[:, None])
    values_raw = keyval[:, 1].reshape(tokens, KVH, HD)
    keys_fresh = keys_rotated.astype(jnp.bfloat16)
    values_fresh = values_raw.astype(jnp.bfloat16)
    queries = lax.optimization_barrier(queries)
    keys_fresh = lax.optimization_barrier(keys_fresh)
    values_fresh = lax.optimization_barrier(values_fresh)
    scaling = 1.0 / math.sqrt(HD)
    key_slots = jnp.arange(MAXP * PAGE, dtype=jnp.int32)
    causal = jnp.arange(Q, dtype=jnp.int32)[:, None] >= jnp.arange(Q, dtype=jnp.int32)[None, :]

    def one_request(request):
        page_ids = jnp.arange(MAXP, dtype=jnp.int32)
        seq_dev = (home_device[request] + page_ids) % N_SEQ
        tensor_dev = request // REQ_DEV
        global_slot = ((seq_dev * N_TENSOR + tensor_dev) * SLOTS_DEV + page_table[request]).astype(jnp.int32)
        cache_keys = k_cache[global_slot].reshape(MAXP * PAGE, KVH, HD).astype(jnp.float32)
        cache_values = v_cache[global_slot].reshape(MAXP * PAGE, KVH, HD).astype(jnp.float32)
        first_row = (request * Q).astype(jnp.int32)
        own_queries = lax.dynamic_slice_in_dim(queries, first_row, Q, 0).astype(jnp.float32)
        own_keys = lax.dynamic_slice_in_dim(keys_fresh, first_row, Q, 0).astype(jnp.float32)
        own_values = lax.dynamic_slice_in_dim(values_fresh, first_row, Q, 0).astype(jnp.float32)
        old_scores = jnp.einsum('qkhd,thd->qkht', own_queries, cache_keys) * scaling
        old_valid = key_slots < lengths[request]
        old_scores = jnp.where(old_valid[None, None, None, :], old_scores, -jnp.inf)
        new_scores = jnp.einsum('qkhd,thd->qkht', own_queries, own_keys) * scaling
        new_scores = jnp.where(causal[:, None, None, :], new_scores, -jnp.inf)
        top_score = jnp.maximum(lax.optimization_barrier(jnp.max(old_scores, axis=-1)), lax.optimization_barrier(jnp.max(new_scores, axis=-1)))
        old_weights = jnp.exp(old_scores - top_score[..., None])
        new_weights = jnp.exp(new_scores - top_score[..., None])
        totals = lax.optimization_barrier(jnp.sum(old_weights, axis=-1)) + lax.optimization_barrier(jnp.sum(new_weights, axis=-1))
        old_rounded = lax.optimization_barrier(old_weights.astype(jnp.bfloat16)).astype(jnp.float32)
        new_rounded = lax.optimization_barrier(new_weights.astype(jnp.bfloat16)).astype(jnp.float32)
        mixture = jnp.einsum('qkht,thd->qkhd', old_rounded, cache_values) + jnp.einsum('qkht,thd->qkhd', new_rounded, own_values)
        return mixture / totals[..., None]
    attended = lax.map(one_request, jnp.arange(REQ, dtype=jnp.int32))
    attended = attended.reshape(tokens, 2, KVH * HD).astype(jnp.bfloat16)
    attended = lax.optimization_barrier(attended)
    chosen = jnp.take_along_axis(router_logits, routes, axis=1)
    gate_probs = jax.nn.softmax(chosen, axis=1)
    projected = jnp.einsum('nkh,ehd->nked', attended.astype(jnp.float32), w_output.astype(jnp.float32))
    mixing = jnp.where(selector, gate_probs[:, :, None], 0.0)
    output = lax.optimization_barrier(jnp.sum(mixing[..., None] * projected, axis=(1, 2)))
    kept_rows = step_of < accepted[request_of]
    attn_out = jnp.where(kept_rows[:, None], output, 0.0)
    new_keys = jnp.where(kept_rows[:, None], keys_rotated.reshape(tokens, KVH * HD), 0.0)
    new_values = jnp.where(kept_rows[:, None], values_raw.reshape(tokens, KVH * HD), 0.0)
    return (attn_out, new_keys, new_values)
```

```python
import functools
import math

import jax
import jax.numpy as jnp
from jax import lax
from jax.experimental import pallas as pl
from jax.experimental.pallas import tpu as pltpu
from jax.sharding import PartitionSpec as P

HD = 128
Q = 4
PAGE = 64
MAXP = 64
CHUNK = 4
TRANSFER = 8 * 2**30


THETA = 10000.0
NEGATIVE = -1e30
VMEM = pl.BlockSpec(memory_space=pltpu.VMEM)
SMEM = pl.BlockSpec(memory_space=pltpu.SMEM)
HBM = pl.BlockSpec(memory_space=pltpu.HBM)
ANY = pl.BlockSpec(memory_space=pl.ANY)


def call(
    body, out_shape, in_specs, *args, out_specs=None, scratch=(), flops=0, moved=0, limit=16
):
    single = not isinstance(out_shape, (list, tuple))
    if out_specs is None:
        out_specs = VMEM if single else [VMEM] * len(out_shape)
    return pl.pallas_call(
        body,
        out_shape=out_shape,
        in_specs=in_specs,
        out_specs=out_specs,
        scratch_shapes=list(scratch),
        compiler_params=pltpu.CompilerParams(vmem_limit_bytes=limit * 2**20),
        cost_estimate=pl.CostEstimate(flops=flops, bytes_accessed=moved, transcendentals=0),
    )(*args)


def in_hbm(array):
    return pltpu.with_memory_space_constraint(array, pltpu.HBM)


def offsets_of(size):
    return [0, *reversed(range(1, size))]


def swapped(blocks, axis, step=1):
    size = lax.axis_size(axis)
    return [
        lax.ppermute(block, axis, [(i, i ^ (d * step)) for i in range(size)]) if d else block
        for d, block in zip(offsets_of(len(blocks)), blocks)
    ]


def neighbour(block):
    size = lax.axis_size("tensor")
    return lax.ppermute(block, "tensor", [(i, i ^ 1) for i in range(size)])


def turned(vectors, cosine, sine):
    return vectors * cosine + pltpu.roll(vectors, HD // 2, 1) * sine


def column_of(row):
    size = row.shape[1]
    place = lax.broadcasted_iota(jnp.int32, (size, size), 0)
    other = lax.broadcasted_iota(jnp.int32, (size, size), 1)
    return jnp.sum(jnp.where(place == other, row, 0.0), axis=1, keepdims=True)


def table_kernel(
    seq_count,
    req_own,
    pages_here,
    routes_ref,
    accepted_ref,
    lengths_ref,
    table_ref,
    home_ref,
    tokens_ref,
    plan_ref,
    routes_buf,
    accepted_buf,
    lengths_buf,
    table_buf,
    home_buf,
    sem,
):
    sources = (routes_ref, accepted_ref, lengths_ref, table_ref, home_ref)
    targets = (routes_buf, accepted_buf, lengths_buf, table_buf, home_buf)
    copies = [
        pltpu.make_async_copy(source, target, sem.at[i])
        for i, (source, target) in enumerate(zip(sources, targets))
    ]
    for copy in copies:
        copy.start()
    for copy in copies:
        copy.wait()
    seq_index = lax.axis_index("seq")
    tensor_index = lax.axis_index("tensor")
    for r in range(req_own):
        request = tensor_index * req_own + r
        offset = (seq_index - home_buf[request] + seq_count) % seq_count
        length = lengths_buf[request]
        pages = ((length + PAGE - 1) // PAGE - offset + seq_count - 1) // seq_count
        plan_ref[r, 0] = (pages + CHUNK - 1) // CHUNK
        plan_ref[r, 1] = length
        plan_ref[r, 2] = offset
        for p in range(pages_here):
            plan_ref[r, 3 + p] = table_buf[request, offset + seq_count * p]
    tokens = tokens_ref.shape[0]
    requests = accepted_ref.shape[1]
    lane = lax.broadcasted_iota(jnp.int32, tokens_ref.shape, 1)
    table = jnp.zeros(tokens_ref.shape, jnp.float32)
    for k in range(2):
        column = column_of(routes_buf[k : k + 1, :].astype(jnp.float32))
        table = jnp.where(lane == k, column, table)
    row = lax.broadcasted_iota(jnp.int32, (tokens, requests), 0)
    request = lax.broadcasted_iota(jnp.int32, (tokens, requests), 1)
    limit = jnp.sum(
        jnp.where(row // Q == request, accepted_buf[...].astype(jnp.float32), 0.0),
        axis=1,
        keepdims=True,
    )
    step = (lax.broadcasted_iota(jnp.int32, (tokens, 1), 0) % Q).astype(jnp.float32)
    table = jnp.where(lane == 2, jnp.where(step < limit, 1.0, 0.0), table)
    tokens_ref[...] = table.astype(jnp.int32)


def project_kernel(seq_count, *refs):
    hidden_refs = refs[:seq_count]
    tokens_ref, query_weight_ref, keyval_weight_ref = refs[seq_count : seq_count + 3]
    keep_ref, give_ref, columns_ref = refs[seq_count + 3 :]
    seq_index = lax.axis_index("seq")
    rows = hidden_refs[0].shape[0]
    for d, hidden_ref in zip(offsets_of(seq_count), hidden_refs):
        start = pl.multiple_of((seq_index ^ d) * rows, rows)
        columns_ref[pl.ds(start, rows), :] = hidden_ref[...]
    columns = columns_ref[...]
    experts, depth, width = query_weight_ref.shape
    weights = query_weight_ref[...].reshape(experts * depth, width)
    masked = []
    for e in range(experts):
        masked.append(
            jnp.concatenate(
                [
                    columns
                    * jnp.where(tokens_ref[:, k : k + 1] == e, 1.0, 0.0).astype(jnp.bfloat16)
                    for k in range(2)
                ],
                axis=0,
            )
        )
    queries = jnp.dot(
        jnp.concatenate(masked, axis=1), weights, preferred_element_type=jnp.float32
    )
    tokens = columns.shape[0]
    parts = [queries[:tokens], queries[tokens:]]
    for c in range(2):
        parts.append(jnp.dot(columns, keyval_weight_ref[c], preferred_element_type=jnp.float32))
    own = keep_ref.shape[1] // 4
    parity = lax.axis_index("tensor") % 2
    for t in range(2 * keep_ref.shape[0]):
        span = slice(t * own, (t + 1) * own)
        block = jnp.concatenate([part[span] for part in parts], axis=0).astype(jnp.bfloat16)

        @pl.when(parity == t % 2)
        def _():
            keep_ref[t // 2] = block

        @pl.when(parity != t % 2)
        def _():
            give_ref[t // 2] = block


def pair_kernel(keep_ref, arrived_ref, *out_refs):
    place = lax.axis_index("tensor") // 2
    for d, out_ref in zip(offsets_of(len(out_refs)), out_refs):
        out_ref[...] = (
            keep_ref[place ^ d].astype(jnp.float32) + arrived_ref[place ^ d].astype(jnp.float32)
        ).astype(jnp.bfloat16)


def total_of(refs, rows=slice(None)):
    return functools.reduce(jnp.add, [ref[rows].astype(jnp.float32) for ref in refs])


def by_request(rows, own):
    return jnp.concatenate(
        [
            rows[k * own + r * Q : k * own + (r + 1) * Q]
            for r in range(own // Q)
            for k in range(2)
        ],
        axis=0,
    )


def by_choice(rows, own):
    return jnp.concatenate(
        [
            rows[(r * 2 + k) * Q : (r * 2 + k + 1) * Q]
            for k in range(2)
            for r in range(own // Q)
        ],
        axis=0,
    )


def turn_kernel(cosine_ref, sine_ref, *refs):
    parts, out_ref = refs[:-1], refs[-1]
    own = out_ref.shape[0] // 2
    total = total_of(parts, slice(0, 2 * own))
    cosine = jnp.concatenate([cosine_ref[...]] * 2, axis=0)
    sine = jnp.concatenate([sine_ref[...]] * 2, axis=0)
    heads = [
        turned(total[:, h * HD : (h + 1) * HD], cosine, sine) for h in range(total.shape[1] // HD)
    ]
    out_ref[...] = by_request(jnp.concatenate(heads, axis=1), own).astype(jnp.bfloat16)


def fresh_kernel(tokens_ref, cosine_ref, sine_ref, query_ref, *refs):
    parts, (keys_ref, values_ref, out_ref) = refs[:-3], refs[-3:]
    tensor_index = lax.axis_index("tensor")
    own = keys_ref.shape[0]
    total = total_of(parts, slice(2 * own, 4 * own))
    heads_here = total.shape[1] // HD
    keys = jnp.concatenate(
        [
            turned(total[:own, h * HD : (h + 1) * HD], cosine_ref[...], sine_ref[...])
            for h in range(heads_here)
        ],
        axis=1,
    )
    values = total[own:]
    start = pl.multiple_of(tensor_index * own, own)
    kept = tokens_ref[pl.ds(start, own), 2:3] > 0
    keys_ref[...] = jnp.where(kept, keys, 0.0)
    values_ref[...] = jnp.where(kept, values, 0.0)
    rows = 2 * own
    query_row = lax.broadcasted_iota(jnp.int32, (rows, own), 0)
    key_row = lax.broadcasted_iota(jnp.int32, (rows, own), 1)
    valid = (query_row // (2 * Q) == key_row // Q) & (query_row % Q >= key_row % Q)
    lane = lax.broadcasted_iota(jnp.int32, (rows, HD), 1)
    notes = jnp.zeros((rows, HD), jnp.float32)
    for h in range(heads_here):
        span = slice(h * HD, (h + 1) * HD)
        scores = lax.dot_general(
            query_ref[:, span],
            keys[:, span].astype(jnp.bfloat16),
            (((1,), (1,)), ((), ())),
            preferred_element_type=jnp.float32,
        ) * (1.0 / math.sqrt(HD))
        scores = jnp.where(valid, scores, NEGATIVE)
        top = jnp.max(scores, axis=1, keepdims=True)
        weights = jnp.where(valid, jnp.exp(scores - top), 0.0)
        sums = jnp.sum(weights, axis=1, keepdims=True)
        mixed = jnp.dot(
            weights.astype(jnp.bfloat16),
            values[:, span].astype(jnp.bfloat16),
            preferred_element_type=jnp.float32,
        )
        out_ref[:, span] = mixed / sums
        notes = jnp.where(lane == h, top + jnp.log(sums), notes)
    out_ref[:, heads_here * HD :] = notes


def cache_kernel(seq_count, req_own, pages_here, plan_ref, *refs):
    query_refs = refs[:seq_count]
    k_buf, v_buf = refs[seq_count : seq_count + 2]
    out_refs = refs[seq_count + 2 : 2 * seq_count + 2]
    query_buf, spread, total_buf, out_buf = refs[2 * seq_count + 2 :]
    seq_index = lax.axis_index("seq")
    width = query_refs[0].shape[1]
    heads_here = width // HD
    kv_heads = heads_here * seq_count
    full = kv_heads * HD
    rows = 2 * Q
    lanes = kv_heads * rows
    chunk_keys = CHUNK * PAGE
    counts = [plan_ref[r, 0] for r in range(req_own)]
    lengths = [plan_ref[r, 1] for r in range(req_own)]
    offsets = [plan_ref[r, 2] for r in range(req_own)]
    for d, query_ref in zip(offsets_of(seq_count), query_refs):
        start = pl.multiple_of((seq_index ^ d) * width, width)
        query_buf[:, pl.ds(start, width)] = query_ref[...].astype(jnp.float32)
    row_head = lax.broadcasted_iota(jnp.int32, (lanes, full), 0) // rows
    column_head = lax.broadcasted_iota(jnp.int32, (lanes, full), 1) // HD
    diagonal = row_head == column_head
    for r in range(req_own):
        wide = jnp.concatenate([query_buf[r * rows : (r + 1) * rows, :full]] * kv_heads, axis=0)
        spread[r] = jnp.where(diagonal, wide, 0.0).T.astype(jnp.bfloat16)

    key_page = lax.broadcasted_iota(jnp.int32, (chunk_keys, lanes), 0) // PAGE
    key_row = lax.broadcasted_iota(jnp.int32, (chunk_keys, lanes), 0) % PAGE
    key_place = key_page * (seq_count * PAGE) + key_row
    for r in range(req_own):

        for count in range(pages_here // CHUNK + 1):

            @pl.when(counts[r] == count)
            def _():
                pairs = full // (2 * HD)
                if count == 0:
                    out_buf[...] = jnp.zeros_like(out_buf)
                    total_buf[...] = jnp.zeros_like(total_buf)
                    return
                slots = [plan_ref[r, 3 + p] for p in range(count * CHUNK)]
                scores = []
                for c in range(count):
                    keys = jnp.concatenate(
                        [k_buf[slot] for slot in slots[c * CHUNK : (c + 1) * CHUNK]], axis=0
                    )
                    score = jnp.dot(keys, spread[r], preferred_element_type=jnp.float32) * (
                        1.0 / math.sqrt(HD)
                    )
                    base = (offsets[r] + seq_count * CHUNK * c) * PAGE
                    scores.append(jnp.where(key_place < lengths[r] - base, score, NEGATIVE))
                top = functools.reduce(
                    jnp.maximum, [jnp.max(score, axis=0, keepdims=True) for score in scores]
                )
                weights = [jnp.exp(score - top) for score in scores]
                total_buf[0:1, :] = top
                total_buf[1:2, :] = functools.reduce(
                    jnp.add, [jnp.sum(weight, axis=0, keepdims=True) for weight in weights]
                )
                flipped = jnp.concatenate(
                    [weight.T.astype(jnp.bfloat16) for weight in weights], axis=1
                )
                for i in range(pairs):
                    span = slice(i * 2 * HD, (i + 1) * 2 * HD)
                    values = jnp.concatenate([v_buf[slot, :, span] for slot in slots], axis=0)
                    out_buf[:, span] = jnp.dot(
                        flipped[i * 2 * rows : (i + 1) * 2 * rows, :],
                        values,
                        preferred_element_type=jnp.float32,
                    )

        top, sums = total_buf[0:1, :], total_buf[1:2, :]
        some = sums > 0.0
        safe = jnp.where(some, sums, 1.0)
        logs = jnp.where(some, top + jnp.log(safe), NEGATIVE)
        inverse = jnp.broadcast_to(1.0 / safe, (HD, lanes)).T
        logs = jnp.broadcast_to(logs, (HD, lanes)).T
        lane = lax.broadcasted_iota(jnp.int32, (rows, HD), 1)
        for g in range(seq_count):
            notes = jnp.zeros((rows, HD), jnp.float32)
            for j in range(heads_here):
                h = g * heads_here + j
                half = (h % 2) * rows
                spread_rows = slice(h * rows, (h + 1) * rows)
                mixed = out_buf[half : half + rows, h * HD : (h + 1) * HD] * inverse[spread_rows]
                query_buf[r * rows : (r + 1) * rows, h * HD : (h + 1) * HD] = mixed
                log = logs[spread_rows]
                high = log.astype(jnp.bfloat16).astype(jnp.float32)
                middle = (log - high).astype(jnp.bfloat16).astype(jnp.float32)
                for part, value in enumerate((high, middle, log - high - middle)):
                    notes = jnp.where(lane == part * heads_here + j, value, notes)
            query_buf[r * rows : (r + 1) * rows, full + g * HD : full + (g + 1) * HD] = notes
    for d, out_ref in zip(offsets_of(seq_count), out_refs):
        group = seq_index ^ d
        start = pl.multiple_of(group * width, width)
        out_ref[:, :width] = query_buf[:, pl.ds(start, width)].astype(jnp.bfloat16)
        start = pl.multiple_of(full + group * HD, HD)
        out_ref[:, width:] = query_buf[:, pl.ds(start, HD)].astype(jnp.bfloat16)


def join_kernel(fresh_ref, *refs):
    parts, out_ref = refs[:-1], refs[-1]
    rows = fresh_ref.shape[0]
    own = rows // 2
    width = out_ref.shape[1]
    heads_here = width // HD
    fresh_notes = fresh_ref[:, width:]
    notes = [part[:, width:].astype(jnp.float32) for part in parts]
    heads = []
    for h in range(heads_here):
        span = slice(h * HD, (h + 1) * HD)
        logs = [fresh_notes[:, h : h + 1]]
        for note in notes:
            logs.append(
                note[:, h : h + 1]
                + note[:, heads_here + h : heads_here + h + 1]
                + note[:, 2 * heads_here + h : 2 * heads_here + h + 1]
            )
        top = functools.reduce(jnp.maximum, logs)
        shares = [jnp.exp(log - top) for log in logs]
        mixed = shares[0] * fresh_ref[:, span]
        for share, part in zip(shares[1:], parts):
            mixed = mixed + share * part[:, span].astype(jnp.float32)
        heads.append(mixed / functools.reduce(jnp.add, shares))
    out_ref[...] = by_choice(jnp.concatenate(heads, axis=1), own).astype(jnp.bfloat16)


def output_kernel(seq_count, tensor_count, tokens_ref, logits_ref, weight_ref, *refs):
    parts = refs[:tensor_count]
    out_refs = refs[tensor_count : tensor_count + seq_count]
    rows_ref, sum_ref = refs[tensor_count + seq_count :]
    seq_index = lax.axis_index("seq")
    tensor_index = lax.axis_index("tensor")
    rows = parts[0].shape[0]
    own = rows // 2
    pairs = [2 * d + half for d in offsets_of(tensor_count // 2) for half in range(2)]
    for d, part in zip(pairs, parts):
        start = pl.multiple_of((tensor_index ^ d) * rows, rows)
        rows_ref[pl.ds(start, rows), :] = part[...]
    experts = weight_ref.shape[0]
    routes = [tokens_ref[:, k : k + 1] for k in range(2)]
    column = lax.broadcasted_iota(jnp.int32, logits_ref.shape, 1)
    logits = logits_ref[...]
    chosen = [
        jnp.sum(jnp.where(column == route, logits, 0.0), axis=1, keepdims=True) for route in routes
    ]
    top = jnp.maximum(chosen[0], chosen[1])
    grown = [jnp.exp(value - top) for value in chosen]
    kept = tokens_ref[:, 2:3] > 0
    gates = [jnp.where(kept, value / (grown[0] + grown[1]), 0.0) for value in grown]
    row_route = jnp.concatenate(
        [routes[k][t * own : (t + 1) * own] for t in range(tensor_count) for k in range(2)], axis=0
    )
    attended = rows_ref[...]
    total = None
    for e in range(experts):
        masked = attended * jnp.where(row_route == e, 1.0, 0.0).astype(jnp.bfloat16)
        product = jnp.dot(masked, weight_ref[e], preferred_element_type=jnp.float32)
        total = product if total is None else total + product
    for t in range(tensor_count):
        span = slice(t * own, (t + 1) * own)
        sum_ref[span, :] = (
            gates[0][span] * total[t * rows : t * rows + own]
            + gates[1][span] * total[t * rows + own : (t + 1) * rows]
        )
    height = out_refs[0].shape[0]
    for d, out_ref in zip(offsets_of(seq_count), out_refs):
        start = pl.multiple_of((seq_index ^ d) * height, height)
        out_ref[...] = sum_ref[pl.ds(start, height), :].astype(out_ref.dtype)


def add_kernel(*refs):
    refs[-1][...] = total_of(refs[:-1])


def per_device(
    hidden,
    router_logits,
    routes,
    w_query,
    w_keyval,
    w_output,
    k_cache,
    v_cache,
    lengths,
    page_table,
    home_device,
    accepted,
):
    seq_count = lax.axis_size("seq")
    tensor_count = lax.axis_size("tensor")
    tok_total = routes.shape[0]
    tok_own = tok_total // tensor_count
    req_own = tok_own // Q
    experts, depth, width = w_query.shape
    out_width = w_output.shape[2]
    heads_here = width // HD
    kv_heads = heads_here * seq_count
    full = kv_heads * HD
    pages_here = MAXP // seq_count
    rows = 2 * tok_own
    height = tok_total // seq_count
    bf16, f32 = jnp.bfloat16, jnp.float32

    def shape(dims, dtype):
        return jax.ShapeDtypeStruct(dims, dtype)

    with jax.named_scope("gather_hidden"):
        hiddens = swapped([hidden] * seq_count, "seq")
    with jax.named_scope("make_tables"):
        tokens, plan = call(
            functools.partial(table_kernel, seq_count, req_own, pages_here),
            [
                shape((tok_total, HD), jnp.int32),
                shape((req_own, 3 + pages_here), jnp.int32),
            ],
            [HBM] * 5,
            in_hbm(routes.T),
            in_hbm(accepted.reshape(1, -1)),
            in_hbm(lengths),
            in_hbm(page_table),
            in_hbm(home_device),
            out_specs=[VMEM, SMEM],
            scratch=[
                pltpu.VMEM((2, tok_total), jnp.int32),
                pltpu.VMEM((1, accepted.shape[0]), jnp.int32),
                pltpu.SMEM(lengths.shape, jnp.int32),
                pltpu.SMEM(page_table.shape, jnp.int32),
                pltpu.SMEM(home_device.shape, jnp.int32),
                pltpu.SemaphoreType.DMA((5,)),
            ],
            flops=TRANSFER,
        )
        keyval_weight = jnp.swapaxes(w_keyval, 0, 1)
    with jax.named_scope("project_tokens"):
        half = shape((tensor_count // 2, 2 * rows, width), bf16)
        keep, give = call(
            functools.partial(project_kernel, seq_count),
            [half] * 2,
            [VMEM] * (seq_count + 3),
            *hiddens,
            tokens,
            w_query,
            keyval_weight,
            scratch=[pltpu.VMEM((tok_total, depth), bf16)],
            flops=2 * TRANSFER,
        )
    with jax.named_scope("sum_tokens"):
        parts = call(
            pair_kernel,
            [shape((2 * rows, width), bf16)] * (tensor_count // 2),
            [VMEM] * 2,
            keep,
            neighbour(give),
        )
        parts = swapped(parts, "tensor", 2)
    with jax.named_scope("rotation_table"):
        positions = jnp.repeat(plan[:, 1], Q) + jnp.arange(tok_own, dtype=jnp.int32) % Q
        inverse = THETA ** (-(jnp.arange(HD // 2, dtype=f32) * 2.0 / HD))
        angles = positions.astype(f32)[:, None] * inverse
        cosine = jnp.cos(angles)
        sine = jnp.sin(angles)
        cosine = jnp.concatenate([cosine, cosine], axis=1)
        sine = jnp.concatenate([-sine, sine], axis=1)
    with jax.named_scope("rotate_queries"):
        queries = call(
            turn_kernel,
            shape((rows, width), bf16),
            [VMEM] * (2 + tensor_count // 2),
            cosine,
            sine,
            *parts,
        )
    with jax.named_scope("gather_queries"):
        queries_all = swapped([queries] * seq_count, "seq")
    with jax.named_scope("attend_fresh"):
        new_keys, new_values, fresh = call(
            fresh_kernel,
            [shape((tok_own, width), f32)] * 2 + [shape((rows, width + HD), f32)],
            [VMEM] * (4 + tensor_count // 2),
            tokens,
            cosine,
            sine,
            queries,
            *parts,
            moved=rows * width * 2 * tensor_count,
        )
    with jax.named_scope("attend_cache"):
        cache_parts = call(
            functools.partial(cache_kernel, seq_count, req_own, pages_here),
            [shape((rows, width + HD), bf16)] * seq_count,
            [SMEM] + [VMEM] * (seq_count + 2),
            plan,
            *queries_all,
            k_cache,
            v_cache,
            scratch=[
                pltpu.VMEM((rows, full + seq_count * HD), f32),
                pltpu.VMEM((req_own, full, kv_heads * 2 * Q), bf16),
                pltpu.VMEM((8, kv_heads * 2 * Q), f32),
                pltpu.VMEM((4 * Q, full), f32),
            ],
            flops=4 * req_own * pages_here * PAGE * full * kv_heads * 2 * Q,
            moved=req_own * pages_here * PAGE * full * 4,
            limit=28,
        )
    with jax.named_scope("trade_partials"):
        cache_parts = swapped(cache_parts, "seq")
    with jax.named_scope("join_partials"):
        attended = call(
            join_kernel,
            shape((rows, width), bf16),
            [VMEM] * (1 + seq_count),
            fresh,
            *cache_parts,
            moved=rows * width * 2 * seq_count,
        )
    with jax.named_scope("gather_attended"):
        far = swapped([attended] * (tensor_count // 2), "tensor", 2)
        attended_all = [part for block in far for part in (block, neighbour(block))]
    with jax.named_scope("project_output"):
        out_parts = call(
            functools.partial(output_kernel, seq_count, tensor_count),
            [shape((height, out_width), bf16)] * seq_count,
            [VMEM] * (3 + tensor_count),
            tokens,
            router_logits,
            w_output,
            *attended_all,
            scratch=[
                pltpu.VMEM((tensor_count * rows, width), bf16),
                pltpu.VMEM((tok_total, out_width), f32),
            ],
            flops=4 * tok_total * experts * width * out_width,
            moved=w_output.size * 2,
        )
    with jax.named_scope("sum_output"):
        out_parts = swapped(out_parts, "seq")
    with jax.named_scope("add_output"):
        attn_out = call(
            add_kernel,
            shape((height, out_width), f32),
            [VMEM] * seq_count,
            *out_parts,
            moved=height * out_width * 2 * seq_count,
        )
    return (attn_out, new_keys, new_values)


def solution(mesh):
    in_specs = (
        P("seq", "tensor"),
        P(),
        P(),
        P(None, "tensor", "seq"),
        P("tensor", None, "seq"),
        P(None, "seq", "tensor"),
        P(("seq", "tensor"), None, None),
        P(("seq", "tensor"), None, None),
        P(),
        P(),
        P(),
        P(),
    )
    out_specs = (P("seq", "tensor"), P("tensor", "seq"), P("tensor", "seq"))
    return jax.shard_map(
        per_device, mesh=mesh, in_specs=in_specs, out_specs=out_specs, check_vma=False
    )
```
